32 devices in a mesh: region: 8 (over z, x), tm: 4 (over y, core).
Axes of the slice: x: 2, y: 2, z: 4, core: 2. Of those that a mesh axis runs over, the one named last changes fastest.
Arguments:
- right_side: float32 [1024, 4096], P('tm', 'region'), may hold values from -9 to 9
- initial: float32 [1024, 4096], P('tm', 'region'), may hold values from -1.5 to 1.5
- blocks: bfloat16 [32, 9, 128, 128], P(('region', 'tm')), may hold values from -2.5 to 3.1, as said below
- neighbour_blocks: int32 [32, 8], P('region'), may hold values from 0 to 31, as said below
- temporal_cov: bfloat16 [1024, 1024], P('tm'), may hold values from -2.5 to 2.8, as said below
Outputs:
- solution: float32 [1024, 4096], P('tm', 'region')
- residual: float32 [1024, 4096], P('tm', 'region')
The draws below stay inside these ranges and needn't reach their ends.
Inputs may be any that keep to these rules, and one draw needn't show every extreme that they name: blocks[i, 0] is symmetric positive definite. `neighbour_blocks`: each column names every block exactly once. Blocks fall into cyclic windows of 4 consecutive blocks starting at 2 + m * 4, and every block listed for row i lies in the window of i. temporal_cov is symmetric positive definite.
All inputs are finite; a program needn't handle non-finite values.
Results may differ from the reference program's by a relative error of at most 0.012.
The reference program's roundings to bfloat16 on the way count: a program that leaves them out, or rounds other values in their place, can miss the bound.
Values may be sent and summed in bfloat16 or wider, within the bound.
A program may use at most 64 MiB of HBM per device.

```python
import jax
import jax.numpy as jnp
from jax import lax

HOURS = 1024
BLK = 128
NBR = 9
ITERS = 2
ROWS_REGION = 4
BLOCKS = 32
SITES = 4096
N_REGION = 8


def draw_right_side(key, part):
    hour_place = (jnp.arange(HOURS, dtype=jnp.float32) / HOURS)[:, None]
    site_place = (jnp.arange(SITES, dtype=jnp.float32) / SITES)[None, :]
    scale_ramp = jnp.sqrt((1.0 + 2.0 * hour_place) * (1.0 + 2.0 * site_place))
    noise_base = jnp.clip(jax.random.normal(key, (HOURS, SITES), jnp.float32), -3.0, 3.0)
    return noise_base * scale_ramp


def draw_blocks(key, part):
    key_diag = jax.random.fold_in(key, 11)
    key_off = jax.random.fold_in(key, 12)
    key_sing = jax.random.fold_in(key, 13)
    raw_diag = jnp.clip(jax.random.normal(key_diag, (BLOCKS, BLK, BLK), jnp.float32), -3.0, 3.0)
    lowest = 0.05
    diagonal = 0.25 * jnp.einsum('nab,ncb->nac', raw_diag, raw_diag, precision=lax.Precision.HIGHEST) / BLK
    diagonal = diagonal + 0.8 * jnp.eye(BLK, dtype=jnp.float32)[None]
    mixing = jax.random.normal(key_off, (BLOCKS, NBR - 1, BLK, BLK), jnp.float32)
    orthogonal, upper_part = jnp.linalg.qr(mixing)
    singular = jax.random.uniform(key_sing, (BLOCKS, NBR - 1, 1, BLK), jnp.float32, lowest, 0.1)
    coupling = orthogonal * singular
    whole = jnp.concatenate([diagonal[:, None], coupling], axis=1)
    return whole.astype(jnp.bfloat16)


def draw_neighbour_blocks(key, part):
    regions = BLOCKS // ROWS_REGION
    half_rows = ROWS_REGION // 2
    block_ids = jnp.arange(BLOCKS, dtype=jnp.int32)
    shifted = jnp.mod(block_ids - half_rows, BLOCKS)
    window = shifted // ROWS_REGION
    within = shifted % ROWS_REGION
    columns = []
    for column in range(NBR - 1):
        window_keys = jax.random.split(jax.random.fold_in(key, 101 + column), regions)
        orders = jax.vmap(lambda one_key: jax.random.permutation(one_key, ROWS_REGION))(window_keys)
        landed = window * ROWS_REGION + orders[window, within].astype(jnp.int32)
        columns.append(jnp.mod(landed + half_rows, BLOCKS))
    return jnp.stack(columns, axis=1).astype(jnp.int32)


def draw_temporal_cov(key, part):
    raw_hours = jnp.clip(jax.random.normal(key, (HOURS, HOURS), jnp.float32), -3.0, 3.0)
    gram = jnp.dot(raw_hours, raw_hours.T, precision=lax.Precision.HIGHEST)
    covariance = 0.25 * gram / HOURS + 0.5 * jnp.eye(HOURS, dtype=jnp.float32)
    return covariance.astype(jnp.bfloat16)


def steps_of(stream_key, shape, pieces, least, top_value):
    def one(position, parts):
        draws = jax.random.uniform(jax.random.fold_in(jax.random.fold_in(stream_key, 6), position), (parts,), jnp.float32, least / len(pieces), top_value / len(pieces))
        return jnp.repeat(jnp.exp(draws), shape[position] // parts).reshape((-1,) + (1,) * (len(shape) - position - 1))

    gain = one(*pieces[0])
    for cut in pieces[1:]:
        gain = gain * one(*cut)
    return gain


def bell_draw(key, dims, spread, limit, cuts=(), kind=jnp.bfloat16):
    values = jax.random.normal(key, dims, jnp.float32) * spread
    if len(cuts) > 0:
        values = steps_of(key, dims, cuts, -0.22, 0.18) * values
    return jnp.clip(values, min=-limit, max=limit).astype(kind)


def setup_inputs(seed: int = 0) -> dict:
    key_list = jax.random.split(jax.random.key(seed), 6)
    right_side = draw_right_side(jax.random.fold_in(key_list[5], 71), 0)
    initial = bell_draw(key_list[1], (HOURS, SITES), 0.25, 1.5, ((0, 4), (1, 8)), jnp.float32)
    blocks = draw_blocks(jax.random.fold_in(key_list[5], 71), 0)
    neighbour_blocks = draw_neighbour_blocks(jax.random.fold_in(key_list[5], 71), 0)
    temporal_cov = draw_temporal_cov(jax.random.fold_in(key_list[5], 71), 0)
    return {"right_side": right_side, "initial": initial, "blocks": blocks, "neighbour_blocks": neighbour_blocks, "temporal_cov": temporal_cov}


def spatial_product(lowered, blocks, neighbour_blocks):
    cell_tiles = lowered.astype(jnp.float32).reshape(HOURS, BLOCKS, BLK)
    itself = jnp.arange(BLOCKS, dtype=jnp.int32)[:, None]
    places = jnp.concatenate([itself, neighbour_blocks.astype(jnp.int32)], axis=1)
    places = places.reshape(N_REGION, ROWS_REGION, NBR)
    grouped = blocks.reshape(N_REGION, ROWS_REGION, NBR, BLK, BLK)

    def one_region(paired):
        region_places, region_blocks = paired
        gathered = jnp.take(cell_tiles, region_places, axis=1)
        return jnp.einsum('hrkb,rkab->hra', gathered, region_blocks.astype(jnp.float32), precision=lax.Precision.HIGHEST)
    per_region = lax.map(one_region, (places, grouped))
    return jnp.transpose(per_region, (1, 0, 2, 3)).reshape(HOURS, SITES)

def operate(current, blocks, neighbour_blocks, temporal_cov):
    lowered = current.astype(jnp.bfloat16)
    spatial = spatial_product(lowered, blocks, neighbour_blocks).astype(jnp.bfloat16)
    blended = jnp.dot(temporal_cov.astype(jnp.float32), spatial.astype(jnp.float32), precision=lax.Precision.HIGHEST)
    return current + blended.astype(jnp.bfloat16).astype(jnp.float32)

def reference(right_side, initial, blocks, neighbour_blocks, temporal_cov):
    solution = initial
    residual = right_side - operate(initial, blocks, neighbour_blocks, temporal_cov)
    direction = residual
    norm_now = jnp.sum(residual * residual)
    for iteration in range(ITERS):
        applied = operate(direction, blocks, neighbour_blocks, temporal_cov)
        step_size = norm_now / jnp.sum(direction * applied)
        solution = solution + step_size * direction
        residual = residual - step_size * applied
        norm_next = jnp.sum(residual * residual)
        direction = residual + norm_next / norm_now * direction
        norm_now = norm_next
    return (solution, residual)
```

```python
import functools

import jax
import jax.numpy as jnp
from jax import lax
from jax.experimental import pallas as pl
from jax.experimental.pallas import tpu as pltpu
from jax.sharding import PartitionSpec as P

ITERS = 2
CORES = 2
MESH = pl.DeviceIdType.MESH
NT = (((1,), (1,)), ((), ()))


def fold(value):
    height, width = value.shape
    tall = jnp.sum(value.reshape(height // 8, 8, width), axis=0)
    total = tall[:, :128]
    for lane in range(128, width, 128):
        total = total + tall[:, lane : lane + 128]
    return total


def total_of(value):
    return jnp.sum(jnp.sum(value, axis=1, keepdims=True), axis=0, keepdims=True)


def kernel(
    regions,
    peers,
    right_ref,
    initial_ref,
    blocks_ref,
    places_ref,
    cov_ref,
    solution_ref,
    residual_ref,
    matrix,
    wide,
    gathered,
    direction,
    image,
    near,
    far,
    halo_send,
    halo_recv,
    matrix_send,
    matrix_recv,
    field_send,
    field_recv,
    near_send,
    near_recv,
    far_send,
    far_recv,
):
    hours, sites = right_ref.shape
    own_rows, slots, tile, _ = blocks_ref.shape
    rows = places_ref.shape[0]
    half = rows // 2
    edge = half * tile
    chips = peers // CORES
    region = lax.axis_index("region")
    peer = lax.axis_index("tm")
    chip = peer // CORES
    core = peer % CORES
    sibling = chip * CORES + (CORES - 1 - core)
    pending = []

    def region_at(step):
        return lax.rem(region + step + regions, regions)

    def peer_at(step):
        return lax.rem(peer + step + peers, peers)

    barrier = pltpu.get_barrier_semaphore()
    for step in range(1, peers):
        pl.semaphore_signal(
            barrier, inc=1, device_id=(region, peer_at(step)), device_id_type=MESH
        )
    for step in range(1, regions):
        pl.semaphore_signal(
            barrier, inc=1, device_id=(region_at(step), peer), device_id_type=MESH
        )

    def copy(source, target, send, recv, device):
        return pltpu.make_async_remote_copy(
            src_ref=source,
            dst_ref=target,
            send_sem=send,
            recv_sem=recv,
            device_id=device,
            device_id_type=MESH,
        )

    def start(*parts):
        made = copy(*parts)
        made.start()
        pending.append(made)

    def await_into(target, send, recv):
        copy(target, target, send, recv, (region, sibling)).wait_recv()

    def rows_of(index, size):
        return pl.ds(pl.multiple_of(index * size, size), size)

    class Gather:
        def __init__(self, view, send, recv):
            self.view, self.send, self.recv = view, send, recv

        def begin(self):
            own = self.view(peer)
            for step in range(1, chips):
                other = lax.rem(chip + step, chips) * CORES + core
                start(own, own, self.send.at[step], self.recv.at[step], (region, other))
            start(own, own, self.send.at[0], self.recv.at[0], (region, sibling))

        def forward(self):
            for step in range(1, chips):
                other = lax.rem(chip - step + chips, chips) * CORES + core
                part = self.view(other)
                await_into(part, self.send.at[step], self.recv.at[step])
                place = chips - 1 + step
                start(part, part, self.send.at[place], self.recv.at[place], (region, sibling))

        def finish(self):
            await_into(self.view(sibling), self.send.at[0], self.recv.at[0])
            for step in range(1, chips):
                other = lax.rem(chip - step + chips, chips) * CORES + (CORES - 1 - core)
                place = chips - 1 + step
                await_into(self.view(other), self.send.at[place], self.recv.at[place])

    def send_halo(turn, value):
        field = wide.at[turn]
        field[:, edge : edge + sites] = value.astype(jnp.bfloat16)
        if turn == 0:
            pl.semaphore_wait(barrier, peers + regions - 2)
        start(
            field.at[:, sites : sites + edge],
            field.at[:, 0:edge],
            halo_send.at[turn, 0],
            halo_recv.at[turn, 0],
            (region_at(1), peer),
        )
        start(
            field.at[:, edge : 2 * edge],
            field.at[:, edge + sites : 2 * edge + sites],
            halo_send.at[turn, 1],
            halo_recv.at[turn, 1],
            (region_at(-1), peer),
        )

    matrix_gather = Gather(
        lambda index: matrix.at[rows_of(index, own_rows * tile), :], matrix_send, matrix_recv
    )

    def build_matrix():
        for own in range(own_rows):
            row = peer * own_rows + own
            shift = jnp.where(row < half, -half, half)
            base = region * rows + shift
            spots = [row - shift]
            for slot in range(slots - 1):
                spots.append(lax.rem(places_ref[row, slot] - base + regions * rows, regions * rows))
            for column in range(rows):
                total = jnp.zeros((tile, tile), jnp.float32)
                for slot in range(slots):
                    weight = jnp.where(spots[slot] == column, 1.0, 0.0).astype(jnp.float32)
                    total = total + weight * blocks_ref[own, slot].astype(jnp.float32)
                matrix[rows_of(row, tile), column * tile : (column + 1) * tile] = total.astype(
                    jnp.bfloat16
                )
        matrix_gather.begin()

    def operate(turn):
        if turn == 0:
            build_matrix()
            matrix_gather.forward()
            matrix_gather.finish()
        field = wide.at[turn]
        gathers = []
        for side in range(2):
            landed = field.at[:, 0:edge] if side == 0 else field.at[:, edge + sites : 2 * edge + sites]
            await_into(landed, halo_send.at[turn, side], halo_recv.at[turn, side])
            spatial = lax.dot_general(
                field[:, side * sites : (side + 1) * sites],
                matrix[side * edge : (side + 1) * edge, :],
                NT,
                preferred_element_type=jnp.float32,
            )
            columns = slice(side * edge, (side + 1) * edge)
            gathered[turn, rows_of(peer, hours), columns] = spatial.astype(jnp.bfloat16)
            gather = Gather(
                lambda index, columns=columns: gathered.at[turn, rows_of(index, hours), columns],
                field_send.at[turn, side],
                field_recv.at[turn, side],
            )
            gather.begin()
            gathers.append(gather)
        for gather in gathers:
            gather.forward()
        for side, gather in enumerate(gathers):
            gather.finish()
            columns = slice(side * edge, (side + 1) * edge)
            temporal = jnp.dot(
                cov_ref[...], gathered[turn, :, columns], preferred_element_type=jnp.float32
            )
            yield columns, temporal.astype(jnp.bfloat16).astype(jnp.float32)

    def reduce(turn, parts):
        count = len(parts) * 8
        for place, part in enumerate(parts):
            near[turn, peer, place * 8 : (place + 1) * 8, :] = part
        own = near.at[turn, peer, 0:count]
        for step in range(1, peers):
            start(own, own, near_send.at[turn, step], near_recv.at[turn, step], (region, peer_at(step)))
        for step in range(1, peers):
            await_into(
                near.at[turn, peer_at(-step), 0:count],
                near_send.at[turn, step],
                near_recv.at[turn, step],
            )
        far[turn, region, 0:count, :] = jnp.sum(near[turn, :, 0:count, :], axis=0)
        own = far.at[turn, region, 0:count]
        for step in range(1, regions):
            start(own, own, far_send.at[turn, step], far_recv.at[turn, step], (region_at(step), peer))
        for step in range(1, regions):
            await_into(
                far.at[turn, region_at(-step), 0:count],
                far_send.at[turn, step],
                far_recv.at[turn, step],
            )
        whole = jnp.sum(far[turn, :, 0:count, :], axis=0)
        return [total_of(whole[place * 8 : (place + 1) * 8]) for place in range(len(parts))]

    send_halo(0, initial_ref[...])
    for columns, temporal in operate(0):
        direction[:, columns] = right_ref[:, columns] - (initial_ref[:, columns] + temporal)
    residual_ref[...] = direction[...]
    solution_ref[...] = initial_ref[...]
    norm = None
    for turn in range(ITERS):
        send_halo(turn + 1, direction[...])
        for columns, temporal in operate(turn + 1):
            image[:, columns] = direction[:, columns] + temporal
        parts = [fold(direction[...] * image[...])]
        if turn + 1 < ITERS:
            parts.append(fold(residual_ref[...] * image[...]))
            parts.append(fold(image[...] * image[...]))
        if turn == 0:
            parts.append(fold(residual_ref[...] * residual_ref[...]))
        sums = reduce(turn, parts)
        if turn == 0:
            norm = sums[-1]
        step_size = norm / sums[0]
        solution_ref[...] = solution_ref[...] + step_size * direction[...]
        residual_ref[...] = residual_ref[...] - step_size * image[...]
        if turn + 1 < ITERS:
            later = norm - 2.0 * step_size * sums[1] + step_size * step_size * sums[2]
            direction[...] = residual_ref[...] + later / norm * direction[...]
            norm = later
    for made in pending:
        made.wait_send()


def local(regions, peers, right_side, initial, blocks, neighbour_blocks, temporal_cov):
    hours, sites = right_side.shape
    rows = neighbour_blocks.shape[0]
    tile = blocks.shape[2]
    turns = ITERS + 1
    dma = pltpu.SemaphoreType.DMA
    vmem = pl.BlockSpec(memory_space=pltpu.VMEM)
    out = jax.ShapeDtypeStruct((hours, sites), jnp.float32)
    width = 2 * sites
    flops = turns * 2 * hours * sites * (rows * tile + temporal_cov.shape[1])
    return pl.pallas_call(
        functools.partial(kernel, regions, peers),
        out_shape=(out, out),
        in_specs=[vmem, vmem, vmem, pl.BlockSpec(memory_space=pltpu.SMEM), vmem],
        out_specs=(vmem, vmem),
        scratch_shapes=[
            pltpu.VMEM((rows * tile, rows * tile), jnp.bfloat16),
            pltpu.VMEM((turns, hours, width), jnp.bfloat16),
            pltpu.VMEM((turns, hours * peers, sites), jnp.bfloat16),
            pltpu.VMEM((hours, sites), jnp.float32),
            pltpu.VMEM((hours, sites), jnp.float32),
            pltpu.VMEM((ITERS, peers, 32, 128), jnp.float32),
            pltpu.VMEM((ITERS, regions, 32, 128), jnp.float32),
            dma((turns, 2)),
            dma((turns, 2)),
            dma((peers - 1,)),
            dma((peers - 1,)),
            dma((turns, 2, peers - 1)),
            dma((turns, 2, peers - 1)),
            dma((ITERS, peers)),
            dma((ITERS, peers)),
            dma((ITERS, regions)),
            dma((ITERS, regions)),
        ],
        compiler_params=pltpu.CompilerParams(
            collective_id=0, has_side_effects=True, vmem_limit_bytes=56 * 1024 * 1024
        ),
        cost_estimate=pl.CostEstimate(flops=flops, bytes_accessed=4 * hours * width, transcendentals=0),
    )(right_side, initial, blocks, neighbour_blocks, temporal_cov)


def solution(mesh):
    in_specs = (
        P("tm", "region"),
        P("tm", "region"),
        P(("region", "tm"), None, None, None),
        P("region", None),
        P("tm", None),
    )
    out_specs = (P("tm", "region"), P("tm", "region"))
    body = functools.partial(local, mesh.shape["region"], mesh.shape["tm"])
    return jax.shard_map(body, mesh=mesh, in_specs=in_specs, out_specs=out_specs, check_vma=False)
```

```python
import functools

import jax
import jax.numpy as jnp
from jax import lax
from jax.experimental import pallas as pl
from jax.experimental.pallas import tpu as pltpu
from jax.sharding import PartitionSpec as P

ITERS = 2
CORES = 2
MESH = pl.DeviceIdType.MESH
NT = (((1,), (1,)), ((), ()))


def fold(value):
    height, width = value.shape
    tall = jnp.sum(value.reshape(height // 8, 8, width), axis=0)
    total = tall[:, :128]
    for lane in range(128, width, 128):
        total = total + tall[:, lane : lane + 128]
    return total


def total_of(value):
    return jnp.sum(jnp.sum(value, axis=1, keepdims=True), axis=0, keepdims=True)


def kernel(
    regions,
    peers,
    right_ref,
    initial_ref,
    blocks_ref,
    places_ref,
    cov_ref,
    solution_ref,
    residual_ref,
    matrix,
    wide,
    gathered,
    direction,
    image,
    near,
    far,
    halo_send,
    halo_recv,
    matrix_send,
    matrix_recv,
    field_send,
    field_recv,
    near_send,
    near_recv,
    far_send,
    far_recv,
):
    hours, sites = right_ref.shape
    own_rows, slots, tile, _ = blocks_ref.shape
    rows = places_ref.shape[0]
    half = rows // 2
    edge = half * tile
    chips = peers // CORES
    region = lax.axis_index("region")
    peer = lax.axis_index("tm")
    chip = peer // CORES
    core = peer % CORES
    sibling = chip * CORES + (CORES - 1 - core)
    pending = []

    def region_at(step):
        return lax.rem(region + step + regions, regions)

    def peer_at(step):
        return lax.rem(peer + step + peers, peers)

    barrier = pltpu.get_barrier_semaphore()
    for step in range(1, peers):
        pl.semaphore_signal(
            barrier, inc=1, device_id=(region, peer_at(step)), device_id_type=MESH
        )
    for step in range(1, regions):
        pl.semaphore_signal(
            barrier, inc=1, device_id=(region_at(step), peer), device_id_type=MESH
        )

    def copy(source, target, send, recv, device):
        return pltpu.make_async_remote_copy(
            src_ref=source,
            dst_ref=target,
            send_sem=send,
            recv_sem=recv,
            device_id=device,
            device_id_type=MESH,
        )

    def start(*parts):
        made = copy(*parts)
        made.start()
        pending.append(made)

    def await_into(target, send, recv):
        copy(target, target, send, recv, (region, sibling)).wait_recv()

    def rows_of(index, size):
        return pl.ds(pl.multiple_of(index * size, size), size)

    class Gather:
        def __init__(self, view, send, recv):
            self.view, self.send, self.recv = view, send, recv

        def begin(self):
            own = self.view(peer)
            for step in range(1, chips):
                other = lax.rem(chip + step, chips) * CORES + core
                start(own, own, self.send.at[step], self.recv.at[step], (region, other))
            start(own, own, self.send.at[0], self.recv.at[0], (region, sibling))

        def forward(self):
            for step in range(1, chips):
                other = lax.rem(chip - step + chips, chips) * CORES + core
                part = self.view(other)
                await_into(part, self.send.at[step], self.recv.at[step])
                place = chips - 1 + step
                start(part, part, self.send.at[place], self.recv.at[place], (region, sibling))

        def finish(self):
            await_into(self.view(sibling), self.send.at[0], self.recv.at[0])
            for step in range(1, chips):
                other = lax.rem(chip - step + chips, chips) * CORES + (CORES - 1 - core)
                place = chips - 1 + step
                await_into(self.view(other), self.send.at[place], self.recv.at[place])

    def send_halo(turn, value):
        field = wide.at[turn]
        field[1] = value[:, 0:edge].astype(jnp.bfloat16)
        field[2] = value[:, edge:sites].astype(jnp.bfloat16)
        if turn == 0:
            pl.semaphore_wait(barrier, peers + regions - 2)
            matrix_gather.begin()
        start(
            field.at[2],
            field.at[0],
            halo_send.at[turn, 0],
            halo_recv.at[turn, 0],
            (region_at(1), peer),
        )
        start(
            field.at[1],
            field.at[3],
            halo_send.at[turn, 1],
            halo_recv.at[turn, 1],
            (region_at(-1), peer),
        )

    matrix_gather = Gather(
        lambda index: matrix.at[pl.ds(index * own_rows, own_rows)], matrix_send, matrix_recv
    )

    def build_matrix():
        for own in range(own_rows):
            row = peer * own_rows + own
            shift = jnp.where(row < half, -half, half)
            base = region * rows + shift
            spots = [row - shift]
            for slot in range(slots - 1):
                spots.append(lax.rem(places_ref[row, slot] - base + regions * rows, regions * rows))
            for column in range(rows):
                total = jnp.zeros((tile, tile), jnp.float32)
                for slot in range(slots):
                    weight = jnp.where(spots[slot] == column, 1.0, 0.0).astype(jnp.float32)
                    total = total + weight * blocks_ref[own, slot].astype(jnp.float32)
                high = total.astype(jnp.bfloat16)
                low = (total - high.astype(jnp.float32)).astype(jnp.bfloat16)
                across = slice(column * tile, (column + 1) * tile)
                matrix[row, 0, :, across] = high
                matrix[row, 1, :, across] = low

    def operate(turn):
        if turn == 0:
            matrix_gather.forward()
            matrix_gather.finish()
        field = wide.at[turn]
        gathers = []
        for side in range(2):
            landed = field.at[3 * side]
            await_into(landed, halo_send.at[turn, side], halo_recv.at[turn, side])
            spatial = jnp.zeros((hours, edge), jnp.float32)
            for level in range(2):
                for piece in range(2):
                    part = matrix[
                        side * half : (side + 1) * half, level, :, piece * edge : (piece + 1) * edge
                    ]
                    spatial = spatial + lax.dot_general(
                        field[2 * side + piece],
                        part.reshape(edge, edge),
                        NT,
                        preferred_element_type=jnp.float32,
                    )
            gathered[turn, side, rows_of(peer, hours)] = spatial.astype(jnp.bfloat16)
            gather = Gather(
                lambda index, side=side: gathered.at[turn, side, rows_of(index, hours)],
                field_send.at[turn, side],
                field_recv.at[turn, side],
            )
            gather.begin()
            gathers.append(gather)
        for gather in gathers:
            gather.forward()
        for side, gather in enumerate(gathers):
            gather.finish()
            columns = slice(side * edge, (side + 1) * edge)
            temporal = jnp.dot(
                cov_ref[...], gathered[turn, side], preferred_element_type=jnp.float32
            )
            yield columns, temporal.astype(jnp.bfloat16).astype(jnp.float32)

    def reduce(turn, parts):
        count = len(parts) * 8
        for place, part in enumerate(parts):
            near[turn, peer, place * 8 : (place + 1) * 8, :] = part
        own = near.at[turn, peer, 0:count]
        for step in range(1, peers):
            start(own, own, near_send.at[turn, step], near_recv.at[turn, step], (region, peer_at(step)))
        for step in range(1, peers):
            await_into(
                near.at[turn, peer_at(-step), 0:count],
                near_send.at[turn, step],
                near_recv.at[turn, step],
            )
        far[turn, region, 0:count, :] = jnp.sum(near[turn, :, 0:count, :], axis=0)
        own = far.at[turn, region, 0:count]
        for step in range(1, regions):
            start(own, own, far_send.at[turn, step], far_recv.at[turn, step], (region_at(step), peer))
        for step in range(1, regions):
            await_into(
                far.at[turn, region_at(-step), 0:count],
                far_send.at[turn, step],
                far_recv.at[turn, step],
            )
        whole = jnp.sum(far[turn, :, 0:count, :], axis=0)
        return [total_of(whole[place * 8 : (place + 1) * 8]) for place in range(len(parts))]

    build_matrix()
    send_halo(0, initial_ref[...])
    for columns, temporal in operate(0):
        direction[:, columns] = right_ref[:, columns] - (initial_ref[:, columns] + temporal)
    residual_ref[...] = direction[...]
    solution_ref[...] = initial_ref[...]
    norm = None
    for turn in range(ITERS):
        send_halo(turn + 1, direction[...])
        for columns, temporal in operate(turn + 1):
            image[:, columns] = direction[:, columns] + temporal
        parts = [fold(direction[...] * image[...])]
        if turn + 1 < ITERS:
            parts.append(fold(residual_ref[...] * image[...]))
            parts.append(fold(image[...] * image[...]))
        if turn == 0:
            parts.append(fold(residual_ref[...] * residual_ref[...]))
        sums = reduce(turn, parts)
        if turn == 0:
            norm = sums[-1]
        step_size = norm / sums[0]
        solution_ref[...] = solution_ref[...] + step_size * direction[...]
        residual_ref[...] = residual_ref[...] - step_size * image[...]
        if turn + 1 < ITERS:
            later = norm - 2.0 * step_size * sums[1] + step_size * step_size * sums[2]
            direction[...] = residual_ref[...] + later / norm * direction[...]
            norm = later
    for made in pending:
        made.wait_send()


def local(regions, peers, right_side, initial, blocks, neighbour_blocks, temporal_cov):
    hours, sites = right_side.shape
    rows = neighbour_blocks.shape[0]
    tile = blocks.shape[2]
    turns = ITERS + 1
    dma = pltpu.SemaphoreType.DMA
    vmem = pl.BlockSpec(memory_space=pltpu.VMEM)
    out = jax.ShapeDtypeStruct((hours, sites), jnp.float32)
    width = 2 * sites
    held = 4 * (rows * tile) ** 2 + 4 * turns * sites * hours * (peers // 2 + 1) + 24 * hours * sites
    flops = turns * 2 * hours * sites * (rows * tile + temporal_cov.shape[1])
    return pl.pallas_call(
        functools.partial(kernel, regions, peers),
        out_shape=(out, out),
        in_specs=[vmem, vmem, vmem, pl.BlockSpec(memory_space=pltpu.SMEM), vmem],
        out_specs=(vmem, vmem),
        scratch_shapes=[
            pltpu.VMEM((rows, 2, tile, rows * tile), jnp.bfloat16),
            pltpu.VMEM((turns, 4, hours, sites // 2), jnp.bfloat16),
            pltpu.VMEM((turns, 2, hours * peers, sites // 2), jnp.bfloat16),
            pltpu.VMEM((hours, sites), jnp.float32),
            pltpu.VMEM((hours, sites), jnp.float32),
            pltpu.VMEM((ITERS, peers, 32, 128), jnp.float32),
            pltpu.VMEM((ITERS, regions, 32, 128), jnp.float32),
            dma((turns, 2)),
            dma((turns, 2)),
            dma((peers - 1,)),
            dma((peers - 1,)),
            dma((turns, 2, peers - 1)),
            dma((turns, 2, peers - 1)),
            dma((ITERS, peers)),
            dma((ITERS, peers)),
            dma((ITERS, regions)),
            dma((ITERS, regions)),
        ],
        compiler_params=pltpu.CompilerParams(
            collective_id=0, has_side_effects=True, vmem_limit_bytes=min(3 * held, 58 << 20)
        ),
        cost_estimate=pl.CostEstimate(flops=flops, bytes_accessed=4 * hours * width, transcendentals=0),
    )(right_side, initial, blocks, neighbour_blocks, temporal_cov)


def solution(mesh):
    in_specs = (
        P("tm", "region"),
        P("tm", "region"),
        P(("region", "tm"), None, None, None),
        P("region", None),
        P("tm", None),
    )
    out_specs = (P("tm", "region"), P("tm", "region"))
    body = functools.partial(local, mesh.shape["region"], mesh.shape["tm"])
    return jax.shard_map(body, mesh=mesh, in_specs=in_specs, out_specs=out_specs, check_vma=False)
```

```python
import functools

import jax
import jax.numpy as jnp
from jax import lax
from jax.experimental import pallas as pl
from jax.experimental.pallas import tpu as pltpu
from jax.sharding import PartitionSpec as P

ITERS = 2
CORES = 2
MESH = pl.DeviceIdType.MESH
NT = (((1,), (1,)), ((), ()))


def fold(value):
    height, width = value.shape
    tall = jnp.sum(value.reshape(height // 8, 8, width), axis=0)
    total = tall[:, :128]
    for lane in range(128, width, 128):
        total = total + tall[:, lane : lane + 128]
    return total


def total_of(value):
    return jnp.sum(jnp.sum(value, axis=1, keepdims=True), axis=0, keepdims=True)


def kernel(
    regions,
    peers,
    right_hbm,
    initial_ref,
    blocks_ref,
    places_ref,
    cov_hbm,
    solution_ref,
    residual_ref,
    matrix,
    wide,
    gathered,
    direction,
    image,
    near,
    far,
    halo_send,
    halo_recv,
    matrix_send,
    matrix_recv,
    field_send,
    field_recv,
    near_send,
    near_recv,
    far_send,
    far_recv,
    right_mem,
    cov_mem,
    load,
    built,
    first,
    offset,
    arrived,
    given,
    back,
    residual,
):
    right_load = pltpu.make_async_copy(right_hbm, right_mem, load.at[0])
    cov_load = pltpu.make_async_copy(cov_hbm, cov_mem, load.at[1])
    right_load.start()
    cov_load.start()
    right_ref, cov_ref = right_mem, cov_mem
    hours, sites = right_ref.shape
    own_rows, slots, tile, _ = blocks_ref.shape
    rows = places_ref.shape[0]
    half = rows // 2
    edge = half * tile
    turns = ITERS + 1
    chips = peers // CORES
    region = lax.axis_index("region")
    peer = lax.axis_index("tm")
    chip = peer // CORES
    core = peer % CORES
    sibling = chip * CORES + (CORES - 1 - core)
    pending = []

    def region_at(step):
        return lax.rem(region + step + regions, regions)

    def peer_at(step):
        return lax.rem(peer + step + peers, peers)

    barrier = pltpu.get_barrier_semaphore()
    for step in range(1, peers):
        pl.semaphore_signal(
            barrier, inc=1, device_id=(region, peer_at(step)), device_id_type=MESH
        )
    for step in range(1, regions):
        pl.semaphore_signal(
            barrier, inc=1, device_id=(region_at(step), peer), device_id_type=MESH
        )

    def copy(source, target, send, recv, device):
        return pltpu.make_async_remote_copy(
            src_ref=source,
            dst_ref=target,
            send_sem=send,
            recv_sem=recv,
            device_id=device,
            device_id_type=MESH,
        )

    def start(*parts):
        made = copy(*parts)
        made.start()
        pending.append(made)

    def await_into(target, send, recv):
        copy(target, target, send, recv, (region, sibling)).wait_recv()

    def rows_of(index, size):
        return pl.ds(pl.multiple_of(index * size, size), size)

    class Gather:
        def __init__(self, view, send, recv):
            self.view, self.send, self.recv = view, send, recv

        def begin(self):
            own = self.view(peer)
            for step in range(1, chips):
                other = lax.rem(chip + step, chips) * CORES + core
                start(own, own, self.send.at[step], self.recv.at[step], (region, other))
            start(own, own, self.send.at[0], self.recv.at[0], (region, sibling))

        def forward(self):
            for step in range(1, chips):
                other = lax.rem(chip - step + chips, chips) * CORES + core
                part = self.view(other)
                await_into(part, self.send.at[step], self.recv.at[step])
                place = chips - 1 + step
                start(part, part, self.send.at[place], self.recv.at[place], (region, sibling))

        def finish(self):
            await_into(self.view(sibling), self.send.at[0], self.recv.at[0])
            for step in range(1, chips):
                other = lax.rem(chip - step + chips, chips) * CORES + (CORES - 1 - core)
                place = chips - 1 + step
                await_into(self.view(other), self.send.at[place], self.recv.at[place])

    lower = peer < peers // 2
    behind = (region_at(-1), peer)
    ahead = (region_at(1), peer)

    def spot(index):
        return pl.ds(lax.rem(index * own_rows + half, rows), own_rows)

    def shift_copy(level):
        return copy(
            built.at[level],
            matrix.at[level, spot(peer)],
            halo_send.at[turns + 2 + level],
            halo_recv.at[turns + 2 + level],
            behind,
        )

    matrix_gathers = [
        Gather(
            lambda index, level=level: matrix.at[level, spot(index)],
            matrix_send.at[level],
            matrix_recv.at[level],
        )
        for level in range(2)
    ]

    def build_matrix():
        for own in range(own_rows):
            row = peer * own_rows + own
            shift = jnp.where(row < half, -half, half)
            base = region * rows + shift
            spots = [row - shift]
            for slot in range(slots - 1):
                spots.append(lax.rem(places_ref[row, slot] - base + regions * rows, regions * rows))
            for column in range(rows):
                total = jnp.zeros((tile, tile), jnp.float32)
                for slot in range(slots):
                    weight = jnp.where(spots[slot] == column, 1.0, 0.0).astype(jnp.float32)
                    total = total + weight * blocks_ref[own, slot].astype(jnp.float32)
                high = total.astype(jnp.bfloat16)
                low = (total - high.astype(jnp.float32)).astype(jnp.bfloat16)
                span = slice(column * tile, (column + 1) * tile)
                built[0, own, :, span] = high
                built[1, own, :, span] = low

        @pl.when(jnp.logical_not(lower))
        def _():
            for level in range(2):
                matrix[level, spot(peer)] = built[level]

    def begin():
        start(first, wide.at[0, 1], halo_send.at[turns], halo_recv.at[turns], behind)

        @pl.when(lower)
        def _():
            for level in range(2):
                shift_copy(level).start()

        start(offset, arrived, halo_send.at[turns + 1], halo_recv.at[turns + 1], behind)
        for level in range(2):

            @pl.when(lower)
            def _():
                shift_copy(level).wait_recv()

            matrix_gathers[level].begin()
        for gather in matrix_gathers:
            gather.forward()

    def operate(turn, meanwhile):
        field = wide.at[turn]
        if turn == 0:
            await_into(field.at[1], halo_send.at[turns], halo_recv.at[turns])
            for gather in matrix_gathers:
                gather.finish()
        gathers = []
        for side in (1, 0):
            spatial = jnp.zeros((hours, edge), jnp.float32)
            for level in range(2):
                for piece in range(2):
                    part = matrix[
                        level, side * half : (side + 1) * half, :, piece * edge : (piece + 1) * edge
                    ]
                    spatial = spatial + lax.dot_general(
                        field[piece],
                        part.reshape(edge, edge),
                        NT,
                        preferred_element_type=jnp.float32,
                    )
            gathered[turn, side, rows_of(peer, hours)] = spatial.astype(jnp.bfloat16)
            gather = Gather(
                lambda index, side=side: gathered.at[turn, side, rows_of(index, hours)],
                field_send.at[turn, side],
                field_recv.at[turn, side],
            )
            gather.begin()
            gathers.append((side, gather))
        meanwhile()
        for side, gather in gathers:
            gather.forward()
        for side, gather in gathers:
            gather.finish()
            temporal = jnp.dot(
                cov_ref[...], gathered[turn, side], preferred_element_type=jnp.float32
            ).astype(jnp.bfloat16)
            if side == 1:
                given[turn] = temporal
                start(given.at[turn], back.at[turn], halo_send.at[turn], halo_recv.at[turn], ahead)
            yield side, temporal.astype(jnp.float32)

    def returned(turn):
        await_into(back.at[turn], halo_send.at[turn], halo_recv.at[turn])
        return back[turn].astype(jnp.float32)

    def reduce(turn, parts):
        count = 8
        packed = [jnp.sum(part, axis=0, keepdims=True) for part in parts]
        packed.append(jnp.zeros((count - len(parts), 128), jnp.float32))
        near[turn, peer] = jnp.concatenate(packed, axis=0)
        own = near.at[turn, peer, 0:count]
        for step in range(1, peers):
            start(own, own, near_send.at[turn, step], near_recv.at[turn, step], (region, peer_at(step)))
        for step in range(1, peers):
            await_into(
                near.at[turn, peer_at(-step), 0:count],
                near_send.at[turn, step],
                near_recv.at[turn, step],
            )
        far[turn, region, 0:count, :] = jnp.sum(near[turn, :, 0:count, :], axis=0)
        own = far.at[turn, region, 0:count]
        for step in range(1, regions):
            start(own, own, far_send.at[turn, step], far_recv.at[turn, step], (region_at(step), peer))
        for step in range(1, regions):
            await_into(
                far.at[turn, region_at(-step), 0:count],
                far_send.at[turn, step],
                far_recv.at[turn, step],
            )
        whole = jnp.sum(far[turn, :, 0:count, :], axis=0)
        return [total_of(whole[place : place + 1]) for place in range(len(parts))]

    build_matrix()
    first[...] = initial_ref[:, 0:edge].astype(jnp.bfloat16)
    wide[0, 0] = initial_ref[:, edge:sites].astype(jnp.bfloat16)
    right_load.wait()
    offset[...] = right_ref[:, 0:edge] - initial_ref[:, 0:edge]
    pl.semaphore_wait(barrier, peers + regions - 2)
    begin()
    solution_ref[...] = initial_ref[...]
    for side, temporal in operate(0, cov_load.wait):
        if side == 1:
            await_into(arrived, halo_send.at[turns + 1], halo_recv.at[turns + 1])
            direction[2] = arrived[...] - temporal
        else:
            direction[1] = right_ref[:, edge:sites] - (initial_ref[:, edge:sites] + temporal)
    residual[1:3] = direction[1:3]

    def late_start():
        value = right_ref[:, 0:edge] - (initial_ref[:, 0:edge] + returned(0))
        direction[0] = value
        residual[0] = value

    def step(part, size, picture):
        moved = direction[part]
        residual[part] = residual[part] - size * picture
        if part < 2:
            span = slice(part * edge, (part + 1) * edge)
            solution_ref[:, span] = solution_ref[:, span] + size * moved

    def turn_to(part, ratio):
        direction[part] = residual[part] + ratio * direction[part]

    def late_step(turn, size):
        step(0, size, direction[0] + returned(turn + 1))

    norm = None
    meanwhile = late_start
    for turn in range(ITERS):
        wide[turn + 1, 0] = direction[1].astype(jnp.bfloat16)
        wide[turn + 1, 1] = direction[2].astype(jnp.bfloat16)
        for side, temporal in operate(turn + 1, meanwhile):
            image[side] = direction[side + 1] + temporal

        def inner(left, right):
            return fold(left[0] * right[0]) + fold(left[1] * right[1])

        moved, rest, picture = direction[1:3], residual[1:3], image[...]
        parts = [inner(moved, picture)]
        if turn + 1 < ITERS:
            parts.append(inner(rest, picture))
            parts.append(inner(picture, picture))
        if turn == 0:
            parts.append(inner(rest, rest))
        sums = reduce(turn, parts)
        if turn == 0:
            norm = sums[-1]
        size = norm / sums[0]
        step(1, size, image[0])
        if turn + 1 < ITERS:
            step(2, size, image[1])
            later = norm - 2.0 * size * sums[1] + size * size * sums[2]
            ratio = later / norm
            turn_to(1, ratio)
            turn_to(2, ratio)
            norm = later

            def meanwhile(turn=turn, size=size, ratio=ratio):
                late_step(turn, size)
                turn_to(0, ratio)
        else:
            late_step(turn, size)
    residual_ref[:, 0:edge] = residual[0]
    residual_ref[:, edge:sites] = residual[1]

    @pl.when(lower)
    def _():
        for level in range(2):
            shift_copy(level).wait_send()

    for made in pending:
        made.wait_send()


def local(regions, peers, right_side, initial, blocks, neighbour_blocks, temporal_cov):
    hours, sites = right_side.shape
    rows = neighbour_blocks.shape[0]
    tile = blocks.shape[2]
    turns = ITERS + 1
    edge = sites // 2
    dma = pltpu.SemaphoreType.DMA
    vmem = pl.BlockSpec(memory_space=pltpu.VMEM)
    hbm = pl.BlockSpec(memory_space=pltpu.HBM)
    out = jax.ShapeDtypeStruct((hours, sites), jnp.float32)
    width = 2 * sites
    held = 4 * (rows * tile) ** 2 + 4 * turns * sites * hours * (peers // 2 + 1) + 24 * hours * sites
    flops = turns * 2 * hours * sites * (rows * tile + temporal_cov.shape[1])
    return pl.pallas_call(
        functools.partial(kernel, regions, peers),
        out_shape=(out, out),
        in_specs=[hbm, vmem, vmem, pl.BlockSpec(memory_space=pltpu.SMEM), hbm],
        out_specs=(vmem, vmem),
        scratch_shapes=[
            pltpu.VMEM((2, rows, tile, rows * tile), jnp.bfloat16),
            pltpu.VMEM((turns, 2, hours, edge), jnp.bfloat16),
            pltpu.VMEM((turns, 2, hours * peers, sites // 2), jnp.bfloat16),
            pltpu.VMEM((3, hours, edge), jnp.float32),
            pltpu.VMEM((2, hours, edge), jnp.float32),
            pltpu.VMEM((ITERS, peers, 8, 128), jnp.float32),
            pltpu.VMEM((ITERS, regions, 8, 128), jnp.float32),
            dma((turns + 4,)),
            dma((turns + 4,)),
            dma((2, peers - 1)),
            dma((2, peers - 1)),
            dma((turns, 2, peers - 1)),
            dma((turns, 2, peers - 1)),
            dma((ITERS, peers)),
            dma((ITERS, peers)),
            dma((ITERS, regions)),
            dma((ITERS, regions)),
            pltpu.VMEM(right_side.shape, right_side.dtype),
            pltpu.VMEM(temporal_cov.shape, temporal_cov.dtype),
            dma((2,)),
            pltpu.VMEM((2, blocks.shape[0], tile, rows * tile), jnp.bfloat16),
            pltpu.VMEM((hours, edge), jnp.bfloat16),
            pltpu.VMEM((hours, edge), jnp.float32),
            pltpu.VMEM((hours, edge), jnp.float32),
            pltpu.VMEM((turns, hours, edge), jnp.bfloat16),
            pltpu.VMEM((turns, hours, edge), jnp.bfloat16),
            pltpu.VMEM((3, hours, edge), jnp.float32),
        ],
        compiler_params=pltpu.CompilerParams(
            collective_id=0, has_side_effects=True, vmem_limit_bytes=58 << 20
        ),
        cost_estimate=pl.CostEstimate(flops=flops, bytes_accessed=4 * hours * width, transcendentals=0),
    )(right_side, initial, blocks, neighbour_blocks, temporal_cov)


def solution(mesh):
    in_specs = (
        P("tm", "region"),
        P("tm", "region"),
        P(("region", "tm"), None, None, None),
        P("region", None),
        P("tm", None),
    )
    out_specs = (P("tm", "region"), P("tm", "region"))
    body = functools.partial(local, mesh.shape["region"], mesh.shape["tm"])
    return jax.shard_map(body, mesh=mesh, in_specs=in_specs, out_specs=out_specs, check_vma=False)
```

```python
import functools

import jax
import jax.numpy as jnp
from jax import lax
from jax.experimental import pallas as pl
from jax.experimental.pallas import tpu as pltpu
from jax.sharding import PartitionSpec as P

ITERS = 2
CORES = 2
MESH = pl.DeviceIdType.MESH
NT = (((1,), (1,)), ((), ()))


def fold(value):
    height, width = value.shape
    tall = jnp.sum(value.reshape(height // 8, 8, width), axis=0)
    total = tall[:, :128]
    for lane in range(128, width, 128):
        total = total + tall[:, lane : lane + 128]
    return total


def total_of(value):
    return jnp.sum(jnp.sum(value, axis=1, keepdims=True), axis=0, keepdims=True)


def kernel(
    regions,
    peers,
    right_hbm,
    initial_ref,
    blocks_ref,
    places_ref,
    cov_hbm,
    solution_ref,
    residual_ref,
    matrix,
    wide,
    gathered,
    direction,
    image,
    near,
    far,
    halo_send,
    halo_recv,
    matrix_send,
    matrix_recv,
    field_send,
    field_recv,
    near_send,
    near_recv,
    far_send,
    far_recv,
    right_mem,
    cov_mem,
    load,
    built,
    first,
    offset,
    arrived,
    given,
    back,
    residual,
):
    right_load = pltpu.make_async_copy(right_hbm, right_mem, load.at[0])
    cov_load = pltpu.make_async_copy(cov_hbm, cov_mem, load.at[1])
    right_load.start()
    cov_load.start()
    right_ref, cov_ref = right_mem, cov_mem
    hours, sites = right_ref.shape
    own_rows, slots, tile, _ = blocks_ref.shape
    rows = places_ref.shape[0]
    half = rows // 2
    edge = half * tile
    turns = ITERS + 1
    chips = peers // CORES
    region = lax.axis_index("region")
    peer = lax.axis_index("tm")
    chip = peer // CORES
    core = peer % CORES
    sibling = chip * CORES + (CORES - 1 - core)
    pending = []

    def region_at(step):
        return lax.rem(region + step + regions, regions)

    def peer_at(step):
        return lax.rem(peer + step + peers, peers)

    barrier = pltpu.get_barrier_semaphore()
    for step in range(1, peers):
        pl.semaphore_signal(
            barrier, inc=1, device_id=(region, peer_at(step)), device_id_type=MESH
        )
    for step in range(1, regions):
        pl.semaphore_signal(
            barrier, inc=1, device_id=(region_at(step), peer), device_id_type=MESH
        )

    def copy(source, target, send, recv, device):
        return pltpu.make_async_remote_copy(
            src_ref=source,
            dst_ref=target,
            send_sem=send,
            recv_sem=recv,
            device_id=device,
            device_id_type=MESH,
        )

    def start(*parts):
        made = copy(*parts)
        made.start()
        pending.append(made)

    def await_into(target, send, recv):
        copy(target, target, send, recv, (region, sibling)).wait_recv()

    def rows_of(index, size):
        return pl.ds(pl.multiple_of(index * size, size), size)

    class Gather:
        def __init__(self, view, send, recv):
            self.view, self.send, self.recv = view, send, recv

        def begin(self):
            own = self.view(peer)
            for step in range(1, chips):
                other = lax.rem(chip + step, chips) * CORES + core
                start(own, own, self.send.at[step], self.recv.at[step], (region, other))
            start(own, own, self.send.at[0], self.recv.at[0], (region, sibling))

        def forward(self):
            for step in range(1, chips):
                other = lax.rem(chip - step + chips, chips) * CORES + core
                part = self.view(other)
                await_into(part, self.send.at[step], self.recv.at[step])
                place = chips - 1 + step
                start(part, part, self.send.at[place], self.recv.at[place], (region, sibling))

        def finish(self):
            await_into(self.view(sibling), self.send.at[0], self.recv.at[0])
            for step in range(1, chips):
                other = lax.rem(chip - step + chips, chips) * CORES + (CORES - 1 - core)
                place = chips - 1 + step
                await_into(self.view(other), self.send.at[place], self.recv.at[place])

    lower = peer < peers // 2
    behind = (region_at(-1), peer)
    ahead = (region_at(1), peer)

    def spot(index):
        return pl.ds(lax.rem(index * own_rows + half, rows), own_rows)

    def shift_copy(level):
        return copy(
            built.at[level],
            matrix.at[level, spot(peer)],
            halo_send.at[turns + 2 + level],
            halo_recv.at[turns + 2 + level],
            behind,
        )

    matrix_gathers = [
        Gather(
            lambda index, level=level: matrix.at[level, spot(index)],
            matrix_send.at[level],
            matrix_recv.at[level],
        )
        for level in range(4)
    ]

    def build_matrix():
        for own in range(own_rows):
            row = peer * own_rows + own
            shift = jnp.where(row < half, -half, half)
            base = region * rows + shift
            spots = [row - shift]
            for slot in range(slots - 1):
                spots.append(lax.rem(places_ref[row, slot] - base + regions * rows, regions * rows))
            for column in range(rows):
                total = jnp.zeros((tile, tile), jnp.float32)
                for slot in range(slots):
                    weight = jnp.where(spots[slot] == column, 1.0, 0.0).astype(jnp.float32)
                    total = total + weight * blocks_ref[own, slot].astype(jnp.float32)
                high = total.astype(jnp.bfloat16)
                low = (total - high.astype(jnp.float32)).astype(jnp.bfloat16)
                piece, place = divmod(column, half)
                span = slice(place * tile, (place + 1) * tile)
                built[piece, own, :, span] = high
                built[2 + piece, own, :, span] = low

        @pl.when(jnp.logical_not(lower))
        def _():
            for level in range(4):
                matrix[level, spot(peer)] = built[level]

    def begin():
        @pl.when(lower)
        def _():
            for level in range(2):
                shift_copy(level).start()

        start(first, wide.at[0, 1], halo_send.at[turns], halo_recv.at[turns], behind)

        @pl.when(lower)
        def _():
            for level in range(2, 4):
                shift_copy(level).start()


        for level in range(4):

            @pl.when(lower)
            def _():
                shift_copy(level).wait_recv()

            matrix_gathers[level].begin()
            if level > 0:
                matrix_gathers[level - 1].forward()
        matrix_gathers[3].forward()

    def operate(turn, meanwhile):
        field = wide.at[turn]
        if turn == 0:
            await_into(field.at[1], halo_send.at[turns], halo_recv.at[turns])
            for gather in matrix_gathers:
                gather.finish()
        gathers = []
        if turn == 0:
            start(offset, arrived, halo_send.at[turns + 1], halo_recv.at[turns + 1], behind)
        for side in (1, 0):
            spatial = jnp.zeros((hours, edge), jnp.float32)
            for level in range(2):
                for piece in range(2):
                    part = matrix[2 * level + piece, side * half : (side + 1) * half]
                    spatial = spatial + lax.dot_general(
                        field[piece],
                        part.reshape(edge, edge),
                        NT,
                        preferred_element_type=jnp.float32,
                    )
            gathered[turn, side, rows_of(peer, hours)] = spatial.astype(jnp.bfloat16)
            gather = Gather(
                lambda index, side=side: gathered.at[turn, side, rows_of(index, hours)],
                field_send.at[turn, side],
                field_recv.at[turn, side],
            )
            gather.begin()
            gathers.append((side, gather))
        meanwhile()
        for side, gather in gathers:
            gather.forward()
        for side, gather in gathers:
            gather.finish()
            temporal = jnp.dot(
                cov_ref[...], gathered[turn, side], preferred_element_type=jnp.float32
            ).astype(jnp.bfloat16)
            if side == 1:
                given[turn] = temporal
                start(given.at[turn], back.at[turn], halo_send.at[turn], halo_recv.at[turn], ahead)
            yield side, temporal.astype(jnp.float32)

    def returned(turn):
        await_into(back.at[turn], halo_send.at[turn], halo_recv.at[turn])
        return back[turn].astype(jnp.float32)

    def reduce(turn, parts):
        count = 8
        packed = [jnp.sum(part, axis=0, keepdims=True) for part in parts]
        packed.append(jnp.zeros((count - len(parts), 128), jnp.float32))
        near[turn, peer] = jnp.concatenate(packed, axis=0)
        own = near.at[turn, peer, 0:count]
        for step in range(1, peers):
            start(own, own, near_send.at[turn, step], near_recv.at[turn, step], (region, peer_at(step)))
        for step in range(1, peers):
            await_into(
                near.at[turn, peer_at(-step), 0:count],
                near_send.at[turn, step],
                near_recv.at[turn, step],
            )
        far[turn, region, 0:count, :] = jnp.sum(near[turn, :, 0:count, :], axis=0)
        own = far.at[turn, region, 0:count]
        for step in range(1, regions):
            start(own, own, far_send.at[turn, step], far_recv.at[turn, step], (region_at(step), peer))
        for step in range(1, regions):
            await_into(
                far.at[turn, region_at(-step), 0:count],
                far_send.at[turn, step],
                far_recv.at[turn, step],
            )
        whole = jnp.sum(far[turn, :, 0:count, :], axis=0)
        return [total_of(whole[place : place + 1]) for place in range(len(parts))]

    build_matrix()
    first[...] = initial_ref[:, 0:edge].astype(jnp.bfloat16)
    wide[0, 0] = initial_ref[:, edge:sites].astype(jnp.bfloat16)
    right_load.wait()
    offset[...] = right_ref[:, 0:edge] - initial_ref[:, 0:edge]
    pl.semaphore_wait(barrier, peers + regions - 2)
    begin()
    solution_ref[...] = initial_ref[...]
    for side, temporal in operate(0, cov_load.wait):
        if side == 1:
            await_into(arrived, halo_send.at[turns + 1], halo_recv.at[turns + 1])
            direction[2] = arrived[...] - temporal
        else:
            direction[1] = right_ref[:, edge:sites] - (initial_ref[:, edge:sites] + temporal)
    residual[1:3] = direction[1:3]

    def late_start():
        value = right_ref[:, 0:edge] - (initial_ref[:, 0:edge] + returned(0))
        direction[0] = value
        residual[0] = value

    def step(part, size, picture):
        moved = direction[part]
        residual[part] = residual[part] - size * picture
        if part < 2:
            span = slice(part * edge, (part + 1) * edge)
            solution_ref[:, span] = solution_ref[:, span] + size * moved

    def turn_to(part, ratio):
        direction[part] = residual[part] + ratio * direction[part]

    def late_step(turn, size):
        step(0, size, direction[0] + returned(turn + 1))

    norm = None
    meanwhile = late_start
    for turn in range(ITERS):
        wide[turn + 1, 0] = direction[1].astype(jnp.bfloat16)
        wide[turn + 1, 1] = direction[2].astype(jnp.bfloat16)
        for side, temporal in operate(turn + 1, meanwhile):
            image[side] = direction[side + 1] + temporal

        def inner(left, right):
            return fold(left[0] * right[0]) + fold(left[1] * right[1])

        moved, rest, picture = direction[1:3], residual[1:3], image[...]
        parts = [inner(moved, picture)]
        if turn + 1 < ITERS:
            parts.append(inner(rest, picture))
            parts.append(inner(picture, picture))
        if turn == 0:
            parts.append(inner(rest, rest))
        sums = reduce(turn, parts)
        if turn == 0:
            norm = sums[-1]
        size = norm / sums[0]
        step(1, size, image[0])
        if turn + 1 < ITERS:
            step(2, size, image[1])
            later = norm - 2.0 * size * sums[1] + size * size * sums[2]
            ratio = later / norm
            turn_to(1, ratio)
            turn_to(2, ratio)
            norm = later

            def meanwhile(turn=turn, size=size, ratio=ratio):
                late_step(turn, size)
                turn_to(0, ratio)
        else:
            late_step(turn, size)
    residual_ref[:, 0:edge] = residual[0]
    residual_ref[:, edge:sites] = residual[1]

    @pl.when(lower)
    def _():
        for level in range(4):
            shift_copy(level).wait_send()

    for made in pending:
        made.wait_send()


def local(regions, peers, right_side, initial, blocks, neighbour_blocks, temporal_cov):
    hours, sites = right_side.shape
    rows = neighbour_blocks.shape[0]
    tile = blocks.shape[2]
    turns = ITERS + 1
    edge = sites // 2
    dma = pltpu.SemaphoreType.DMA
    vmem = pl.BlockSpec(memory_space=pltpu.VMEM)
    hbm = pl.BlockSpec(memory_space=pltpu.HBM)
    out = jax.ShapeDtypeStruct((hours, sites), jnp.float32)
    width = 2 * sites
    held = 4 * (rows * tile) ** 2 + 4 * turns * sites * hours * (peers // 2 + 1) + 24 * hours * sites
    flops = turns * 2 * hours * sites * (rows * tile + temporal_cov.shape[1])
    return pl.pallas_call(
        functools.partial(kernel, regions, peers),
        out_shape=(out, out),
        in_specs=[hbm, vmem, vmem, pl.BlockSpec(memory_space=pltpu.SMEM), hbm],
        out_specs=(vmem, vmem),
        scratch_shapes=[
            pltpu.VMEM((4, rows, tile, edge), jnp.bfloat16),
            pltpu.VMEM((turns, 2, hours, edge), jnp.bfloat16),
            pltpu.VMEM((turns, 2, hours * peers, sites // 2), jnp.bfloat16),
            pltpu.VMEM((3, hours, edge), jnp.float32),
            pltpu.VMEM((2, hours, edge), jnp.float32),
            pltpu.VMEM((ITERS, peers, 8, 128), jnp.float32),
            pltpu.VMEM((ITERS, regions, 8, 128), jnp.float32),
            dma((turns + 6,)),
            dma((turns + 6,)),
            dma((4, peers - 1)),
            dma((4, peers - 1)),
            dma((turns, 2, peers - 1)),
            dma((turns, 2, peers - 1)),
            dma((ITERS, peers)),
            dma((ITERS, peers)),
            dma((ITERS, regions)),
            dma((ITERS, regions)),
            pltpu.VMEM(right_side.shape, right_side.dtype),
            pltpu.VMEM(temporal_cov.shape, temporal_cov.dtype),
            dma((2,)),
            pltpu.VMEM((4, blocks.shape[0], tile, edge), jnp.bfloat16),
            pltpu.VMEM((hours, edge), jnp.bfloat16),
            pltpu.VMEM((hours, edge), jnp.float32),
            pltpu.VMEM((hours, edge), jnp.float32),
            pltpu.VMEM((turns, hours, edge), jnp.bfloat16),
            pltpu.VMEM((turns, hours, edge), jnp.bfloat16),
            pltpu.VMEM((3, hours, edge), jnp.float32),
        ],
        compiler_params=pltpu.CompilerParams(
            collective_id=0, has_side_effects=True, vmem_limit_bytes=58 << 20
        ),
        cost_estimate=pl.CostEstimate(flops=flops, bytes_accessed=4 * hours * width, transcendentals=0),
    )(right_side, initial, blocks, neighbour_blocks, temporal_cov)


def solution(mesh):
    in_specs = (
        P("tm", "region"),
        P("tm", "region"),
        P(("region", "tm"), None, None, None),
        P("region", None),
        P("tm", None),
    )
    out_specs = (P("tm", "region"), P("tm", "region"))
    body = functools.partial(local, mesh.shape["region"], mesh.shape["tm"])
    return jax.shard_map(body, mesh=mesh, in_specs=in_specs, out_specs=out_specs, check_vma=False)
```
